32 devices in a mesh: leaf: 8 (over y, x, core), grp: 4 (over z).
Axes of the slice: x: 2, y: 2, z: 4, core: 2. Of those that a mesh axis runs over, the one named last changes fastest.
Arguments:
- root_inverse: float32 [512, 512], P(('leaf', 'grp'))
- child_tiles: int32 [8, 8], P('leaf'), may hold values from 0 to 7, as said below
- tile_valid: int32 [8, 8], P('leaf'), may hold values 0 or 1
- factor_off: float32 [8, 512, 512], P('leaf'), may hold values from -0.75 to 0.75
- diag_inverse_t: float32 [8, 512, 512], P('leaf', 'grp')
Outputs:
- cross_blocks: float32 [8, 512, 512], P('leaf', 'grp')
- diagonal_blocks: float32 [8, 512, 512], P('leaf', 'grp')
The draws below stay inside these ranges and needn't reach their ends.
Inputs may be any that keep to these rules, and one draw needn't show every extreme that they name: `child_tiles`: each row lists 8 different tiles.
All inputs are finite; a program needn't handle non-finite values. No bound on the sum of `tile_valid` on one device may be relied on, other than what follows from the above.
Results may differ from the reference program's by a relative error of at most 0.0003.
Values sent between devices are 32-bit elements; how exact they have to be, the bound alone decides.
A program may use at most 128 MiB of HBM per device.

```python
import math
import jax
import jax.numpy as jnp
from jax import lax

B = 64
K = 8
NC = 512
NT = 8
CHILDREN = 8


def draw_root_inverse(key, part):
    key = jax.random.fold_in(key, 1)
    first, second = jax.random.split(key)
    total = NT * B
    raw = jax.random.normal(first, (total, total), jnp.float32)
    diag = jnp.exp(jax.random.uniform(second, (total,), jnp.float32, 0.0, math.log(3.0)))
    rows = jnp.arange(total)[:, None]
    cols = jnp.arange(total)[None, :]
    off = (raw + raw.T) * (0.35 / math.sqrt(total))
    return jnp.where(rows == cols, diag[:, None], off).astype(jnp.float32)


def draw_child_tiles(key, part):
    key = jax.random.fold_in(key, 2)
    keys = jax.random.split(key, CHILDREN)
    chosen = jax.vmap(lambda single: jax.random.permutation(single, NT)[:K])(keys)
    return chosen.astype(jnp.int32)


def draw_diag_inverse_t(key, part):
    key = jax.random.fold_in(key, 3)
    first, second = jax.random.split(key)
    raw = jax.random.normal(first, (CHILDREN, NC, NC), jnp.float32)
    diag = jnp.exp(jax.random.uniform(second, (CHILDREN, NC, 1), jnp.float32, math.log(0.5), math.log(2.0)))
    rows = jnp.arange(NC)[:, None]
    cols = jnp.arange(NC)[None, :]
    upper = jnp.where(cols > rows, raw * (0.6 / math.sqrt(NC)), 0.0)
    return (upper + jnp.where(cols == rows, diag, 0.0)).astype(jnp.float32)


def set_ends(values, key, smallest, high):
    shape = values.shape
    index_at = [jax.random.randint(jax.random.fold_in(key, axis), (), 0, shape[axis]) for axis in range(len(shape))]
    values = values.at[tuple(index_at)].set(smallest)
    longest = shape.index(max(shape))
    index_at[longest] = (index_at[longest] + 1) % shape[longest]
    return values.at[tuple(index_at)].set(high)


def shard_levels(stream_key, shape, pieces, smallest, top_value):
    def one(position, parts):
        draws = jax.random.uniform(jax.random.fold_in(jax.random.fold_in(stream_key, 6), position), (parts,), jnp.float32, smallest / len(pieces), top_value / len(pieces))
        return jnp.repeat(jnp.exp(draws), shape[position] // parts).reshape((-1,) + (1,) * (len(shape) - position - 1))

    loudness = one(*pieces[0])
    for cut in pieces[1:]:
        loudness = loudness * one(*cut)
    return loudness


def scatter_about(key, dims, width, bound, cuts=(), kind=jnp.bfloat16):
    values = width * jax.random.normal(key, dims, jnp.float32)
    if cuts:
        values = values * shard_levels(key, dims, cuts, -0.22, 0.18)
    return jnp.clip(values, -bound, bound).astype(kind)


def setup_inputs(seed: int = 0) -> dict:
    arg_keys = jax.random.split(jax.random.key(seed), 6)
    return {
        "root_inverse": draw_root_inverse(jax.random.fold_in(arg_keys[5], 71), 0),
        "child_tiles": draw_child_tiles(jax.random.fold_in(arg_keys[5], 71), 0),
        "tile_valid": set_ends((jax.random.randint(arg_keys[2], (CHILDREN, K), 0, 4) < 3).astype(jnp.int32), jax.random.fold_in(arg_keys[2], 1), 0, 1),
        "factor_off": scatter_about(arg_keys[3], (CHILDREN, K * B, NC), B ** -0.5, 0.75, ((0, 8),), jnp.float32),
        "diag_inverse_t": draw_diag_inverse_t(jax.random.fold_in(arg_keys[5], 71), 0),
    }


def reference(root_inverse, child_tiles, tile_valid, factor_off, diag_inverse_t):
    highest = lax.Precision.HIGHEST
    offsets = jnp.arange(B, dtype=jnp.int32)

    def one_child(items):
        tile_ids, valid, factor, inverse_t = items
        flat_rows = (tile_ids[:, None] * B + offsets[None, :]).reshape(K * B).astype(jnp.int32)
        row_mask = jnp.repeat(valid.astype(jnp.float32), B)
        masked_factor = factor * row_mask[:, None]
        picked = root_inverse[flat_rows[:, None], flat_rows[None, :]]
        product = jnp.dot(inverse_t, masked_factor.T, precision=highest)
        cross = -jnp.dot(product, picked, precision=highest) * row_mask[None, :]
        q_rows = inverse_t - jnp.dot(cross, masked_factor, precision=highest)
        closing = jnp.dot(q_rows, inverse_t.T, precision=highest)
        return cross, closing

    cross_blocks, diagonal_blocks = lax.map(one_child, (child_tiles, tile_valid, factor_off, diag_inverse_t))
    return cross_blocks, diagonal_blocks
```

```python
import functools

import jax
import jax.numpy as jnp
from jax import lax
from jax.experimental import pallas as pl
from jax.experimental.pallas import tpu as pltpu
from jax.sharding import PartitionSpec as P

B = 64
CHUNKS = 4
MESH = pl.DeviceIdType.MESH
BF16 = jnp.bfloat16
F32 = jnp.float32


def halves(x):
    high = x.astype(BF16)
    return high, (x - high.astype(F32)).astype(BF16)


def dot(a, b, transpose_b=False):
    dims = (((1,), (1 if transpose_b else 0,)), ((), ()))
    return lax.dot_general(a, b, dims, preferred_element_type=F32)


def dot3(a, b, transpose_b=False):
    (ah, al), (bh, bl) = a, b
    return dot(ah, bh, transpose_b) + (dot(al, bh, transpose_b) + dot(ah, bl, transpose_b))


def kernel(
    leaves, groups,
    tiles, valid, root, factor, diag_t, cross_out, closing_out,
    d_all, root_all, f_all, closing,
    local_sem, root_recv, root_zsend, root_psend, root_tsend, d_recv, d_send,
):
    leaf = lax.axis_index("leaf")
    g = lax.axis_index("grp")
    chips = leaves // 2
    chip, core = leaf // 2, lax.rem(leaf, 2)
    twin = chip * 2 + (1 - core)
    listed = tiles.shape[1]
    rows, width = diag_t.shape
    total = root.shape[1]
    part = rows // CHUNKS

    def leaf_of(step):
        return lax.rem(chip + step, chips) * 2 + core

    barrier = pltpu.get_barrier_semaphore()

    @pl.when(g > 0)
    def _():
        pl.semaphore_signal(barrier, inc=1, device_id={"grp": g - 1}, device_id_type=MESH)

    @pl.when(g < groups - 1)
    def _():
        pl.semaphore_signal(barrier, inc=1, device_id={"grp": g + 1}, device_id_type=MESH)

    pl.semaphore_signal(barrier, inc=1, device_id={"leaf": twin}, device_id_type=MESH)
    for step in range(1, chips):
        pl.semaphore_signal(barrier, inc=1, device_id={"leaf": leaf_of(step)}, device_id_type=MESH)

    mine = leaf * groups + g
    copy_d = pltpu.make_async_copy(diag_t, d_all.at[g], local_sem.at[0])
    copy_f = pltpu.make_async_copy(factor, f_all, local_sem.at[1])
    copy_r = pltpu.make_async_copy(root, root_all.at[mine], local_sem.at[2])
    copy_d.start()
    copy_f.start()
    copy_r.start()
    near = jnp.where(g > 0, 1, 0) + jnp.where(g < groups - 1, 1, 0)
    pl.semaphore_wait(barrier, near + chips)

    def root_z(way, owner, own):
        slot = leaf * groups + owner
        return pltpu.make_async_remote_copy(
            src_ref=root if own else root_all.at[slot],
            dst_ref=root_all.at[slot],
            send_sem=root_zsend.at[way, owner],
            recv_sem=root_recv.at[slot],
            device_id={"grp": g + 1 if way == 0 else g - 1},
            device_id_type=MESH,
        )

    def root_plane(step, owner, own):
        slot = leaf * groups + owner
        return pltpu.make_async_remote_copy(
            src_ref=root if own else root_all.at[slot],
            dst_ref=root_all.at[slot],
            send_sem=root_psend.at[step, owner],
            recv_sem=root_recv.at[slot],
            device_id={"leaf": twin if step == 0 else leaf_of(step)},
            device_id_type=MESH,
        )

    def root_twin(step, owner):
        slot = leaf_of(step) * groups + owner
        return pltpu.make_async_remote_copy(
            src_ref=root_all.at[slot],
            dst_ref=root_all.at[slot],
            send_sem=root_tsend.at[step, owner],
            recv_sem=root_recv.at[slot],
            device_id={"leaf": twin},
            device_id_type=MESH,
        )

    def root_arrived(slot):
        pltpu.make_async_remote_copy(
            src_ref=root_all.at[slot],
            dst_ref=root_all.at[slot],
            send_sem=root_tsend.at[0, 0],
            recv_sem=root_recv.at[slot],
            device_id={"leaf": twin},
            device_id_type=MESH,
        ).wait_recv()

    def d_copy(way, owner, c, own):
        piece = pl.ds(c * part, part)
        return pltpu.make_async_remote_copy(
            src_ref=diag_t.at[piece] if own else d_all.at[owner, piece],
            dst_ref=d_all.at[owner, piece],
            send_sem=d_send.at[way, owner, c],
            recv_sem=d_recv.at[owner, c],
            device_id={"grp": g + 1 if way == 0 else g - 1},
            device_id_type=MESH,
        )

    def d_arrived(owner, c):
        piece = pl.ds(c * part, part)
        pltpu.make_async_remote_copy(
            src_ref=d_all.at[owner, piece],
            dst_ref=d_all.at[owner, piece],
            send_sem=d_send.at[0, owner, c],
            recv_sem=d_recv.at[owner, c],
            device_id={"leaf": twin},
            device_id_type=MESH,
        ).wait_recv()

    up, down = g < groups - 1, g > 0

    @pl.when(up)
    def _():
        root_z(0, g, True).start()

    @pl.when(down)
    def _():
        root_z(1, g, True).start()

    for step in list(range(1, chips)) + [0]:
        root_plane(step, g, True).start()
    for c in range(CHUNKS):
        @pl.when(up)
        def _():
            d_copy(0, g, c, True).start()

        @pl.when(down)
        def _():
            d_copy(1, g, c, True).start()

    def forward_root(step):
        for way, owner, there, onward in (
            (0, g - step, g - step >= 0, up),
            (1, g + step, g + step < groups, down),
        ):
            @pl.when(there)
            def _():
                root_arrived(leaf * groups + owner)

                @pl.when(onward)
                def _():
                    root_z(way, owner, False).start()

                for hop in list(range(1, chips)) + [0]:
                    root_plane(hop, owner, False).start()

    def forward_d(step):
        for c in range(CHUNKS):
            for way, owner, there, onward in (
                (0, g - step, g - step >= 0, up),
                (1, g + step, g + step < groups, down),
            ):
                @pl.when(there)
                def _():
                    d_arrived(owner, c)

                    @pl.when(onward)
                    def _():
                        d_copy(way, owner, c, False).start()

    row_at = lax.broadcasted_iota(jnp.int32, (listed * B, 1), 0)
    col_at = lax.broadcasted_iota(jnp.int32, (1, listed * B), 1)
    start = jnp.zeros((listed * B, 1), jnp.int32)
    keep = jnp.zeros((1, listed * B), jnp.int32)
    for k in range(listed):
        met = valid[0, k]
        column = jnp.where(met > 0, tiles[0, k] * B - k * B, -(2 * total) - listed * B)
        start = jnp.where(row_at // B == k, column, start)
        keep = jnp.where(col_at // B == k, met, keep)
    spot = lax.broadcasted_iota(jnp.int32, (listed * B, total), 1)
    pick = (start + row_at == spot).astype(F32)
    chosen = jnp.max(pick, axis=0, keepdims=True) > 0
    pick = pick.astype(BF16)

    copy_d.wait()
    d_own = d_all[g]
    d_half = halves(d_own)
    copy_f.wait()
    f_half = halves(f_all[...])
    product = dot3(d_half, f_half, True)
    product = jnp.where(keep > 0, product, 0.0)
    spread = tuple(dot(x, pick).astype(BF16) for x in halves(product))

    copy_r.wait()
    for step in range(1, groups):
        forward_root(step)
    if groups > 2:
        forward_d(1)
    order = [0]
    for away in range(1, groups):
        order += [away, -away]
    for away in order:
        owner = g + away
        @pl.when(jnp.logical_and(owner >= 0, owner < groups))
        def _():
            for step in range(1, chips):
                root_arrived(leaf_of(step) * groups + owner)
                root_twin(step, owner).start()
    for away in order:
        owner = g + away
        @pl.when(jnp.logical_and(owner >= 0, owner < groups))
        def _():
            for step in range(chips):
                other = lax.rem(chip + step, chips) * 2 + (1 - core)
                root_arrived(other * groups + owner)

    cross = jnp.zeros((rows, listed * B), F32)
    block = min(total, 512)
    for n in range(total // block):
        cols = slice(n * block, (n + 1) * block)
        source = root_all[:, :, cols].reshape(total, block)
        y = dot3(spread, halves(source))
        yh, yl = halves(jnp.where(chosen[:, cols], y, 0.0))
        cross = cross - (dot(yh, pick[:, cols], True) + dot(yl, pick[:, cols], True))
    cross_out[...] = cross
    q = halves(d_own - dot3(halves(cross), f_half))

    def close(owner):
        closing[owner] = dot3(q, halves(d_all[owner]), True)

    close(g)
    for step in range(1, groups):
        if step > 1 or groups <= 2:
            forward_d(step)
        for owner, there in ((g - step, g - step >= 0), (g + step, g + step < groups)):
            @pl.when(there)
            def _():
                close(owner)
    for h in range(groups):
        closing_out[:, h * rows:(h + 1) * rows] = closing[h]

    for h in range(groups):
        for way, goes in (
            (0, jnp.logical_and(h <= g, up)),
            (1, jnp.logical_and(h >= g, down)),
        ):
            @pl.when(goes)
            def _():
                root_z(way, h, False).wait_send()
                for c in range(CHUNKS):
                    d_copy(way, h, c, False).wait_send()
        for step in range(chips):
            root_plane(step, h, False).wait_send()
        for step in range(1, chips):
            root_twin(step, h).wait_send()


def on_device(root, tiles, valid, factor, diag_t):
    leaves, groups = lax.axis_size("leaf"), lax.axis_size("grp")
    rows, width = diag_t.shape[1:]
    part, total = root.shape
    deep = factor.shape[1]
    smem = pl.BlockSpec(memory_space=pltpu.SMEM)
    anywhere = pl.BlockSpec(memory_space=pl.ANY)
    vmem = pl.BlockSpec(memory_space=pltpu.VMEM)
    dma = pltpu.SemaphoreType.DMA
    cross, closing = pl.pallas_call(
        functools.partial(kernel, leaves, groups),
        out_shape=(
            jax.ShapeDtypeStruct((rows, deep), F32),
            jax.ShapeDtypeStruct((rows, groups * rows), F32),
        ),
        in_specs=[smem, smem, anywhere, anywhere, anywhere],
        out_specs=(vmem, vmem),
        scratch_shapes=[
            pltpu.VMEM((groups, rows, width), F32),
            pltpu.VMEM((leaves * groups, part, total), F32),
            pltpu.VMEM((deep, width), F32),
            pltpu.VMEM((groups, rows, rows), F32),
            dma((3,)),
            dma((leaves * groups,)),
            dma((2, groups)),
            dma((leaves // 2, groups)),
            dma((leaves // 2, groups)),
            dma((groups, CHUNKS)),
            dma((2, groups, CHUNKS)),
        ],
        compiler_params=pltpu.CompilerParams(
            collective_id=0, has_side_effects=True, vmem_limit_bytes=56 * 1024 * 1024
        ),
        name="selected_inverse",
    )(tiles, valid, root, factor[0], diag_t[0])
    return cross[None], closing[None]


def solution(mesh):
    in_specs = (
        P(("leaf", "grp"), None),
        P("leaf", None),
        P("leaf", None),
        P("leaf", None, None),
        P("leaf", "grp", None),
    )
    out_specs = (P("leaf", "grp", None), P("leaf", "grp", None))
    return jax.shard_map(
        on_device, mesh=mesh, in_specs=in_specs, out_specs=out_specs, check_vma=False
    )
```

```python
import functools

import jax
import jax.numpy as jnp
from jax import lax
from jax.experimental import pallas as pl
from jax.experimental.pallas import tpu as pltpu
from jax.sharding import PartitionSpec as P

B = 64
CHUNKS = 4
MESH = pl.DeviceIdType.MESH
BF16 = jnp.bfloat16
F32 = jnp.float32


def halves(x):
    high = x.astype(BF16)
    return high, (x - high.astype(F32)).astype(BF16)


def dot(a, b, transpose_b=False):
    dims = (((1,), (1 if transpose_b else 0,)), ((), ()))
    return lax.dot_general(a, b, dims, preferred_element_type=F32)


def dot3(a, b, transpose_b=False):
    (ah, al), (bh, bl) = a, b
    return dot(ah, bh, transpose_b) + (dot(al, bh, transpose_b) + dot(ah, bl, transpose_b))


def kernel(
    leaves, groups,
    tiles, valid, root, factor, diag_t, cross_out, closing_out,
    d_all, root_all, f_all, closing,
    local_sem, root_recv, root_zsend, root_psend, root_tsend, d_recv, d_send,
):
    leaf = lax.axis_index("leaf")
    g = lax.axis_index("grp")
    chips = leaves // 2
    chip, core = leaf // 2, lax.rem(leaf, 2)
    twin = chip * 2 + (1 - core)
    listed = tiles.shape[1]
    rows, width = diag_t.shape
    total = root.shape[1]
    part = rows // CHUNKS

    def leaf_of(step):
        return lax.rem(chip + step, chips) * 2 + core

    barrier = pltpu.get_barrier_semaphore()

    for step in range(1, groups):
        pl.semaphore_signal(
            barrier, inc=1, device_id={"grp": lax.rem(g + step, groups)}, device_id_type=MESH
        )
    pl.semaphore_signal(barrier, inc=1, device_id={"leaf": twin}, device_id_type=MESH)
    for step in range(1, chips):
        pl.semaphore_signal(barrier, inc=1, device_id={"leaf": leaf_of(step)}, device_id_type=MESH)

    mine = leaf * groups + g
    copy_d = pltpu.make_async_copy(diag_t, d_all.at[g], local_sem.at[0])
    copy_f = pltpu.make_async_copy(factor, f_all, local_sem.at[1])
    copy_r = pltpu.make_async_copy(root, root_all.at[mine], local_sem.at[2])
    copy_d.start()
    copy_f.start()
    copy_r.start()
    pl.semaphore_wait(barrier, groups - 1 + chips)

    def root_z(step):
        return pltpu.make_async_remote_copy(
            src_ref=root,
            dst_ref=root_all.at[mine],
            send_sem=root_zsend.at[step],
            recv_sem=root_recv.at[mine],
            device_id={"grp": lax.rem(g + step, groups)},
            device_id_type=MESH,
        )

    def root_plane(step, owner, own):
        slot = leaf * groups + owner
        return pltpu.make_async_remote_copy(
            src_ref=root if own else root_all.at[slot],
            dst_ref=root_all.at[slot],
            send_sem=root_psend.at[step, owner],
            recv_sem=root_recv.at[slot],
            device_id={"leaf": twin if step == 0 else leaf_of(step)},
            device_id_type=MESH,
        )

    def root_twin(step, owner):
        slot = leaf_of(step) * groups + owner
        return pltpu.make_async_remote_copy(
            src_ref=root_all.at[slot],
            dst_ref=root_all.at[slot],
            send_sem=root_tsend.at[step, owner],
            recv_sem=root_recv.at[slot],
            device_id={"leaf": twin},
            device_id_type=MESH,
        )

    def root_arrived(slot):
        pltpu.make_async_remote_copy(
            src_ref=root_all.at[slot],
            dst_ref=root_all.at[slot],
            send_sem=root_tsend.at[0, 0],
            recv_sem=root_recv.at[slot],
            device_id={"leaf": twin},
            device_id_type=MESH,
        ).wait_recv()

    def d_copy(way, owner, c, own):
        piece = pl.ds(c * part, part)
        return pltpu.make_async_remote_copy(
            src_ref=diag_t.at[piece] if own else d_all.at[owner, piece],
            dst_ref=d_all.at[owner, piece],
            send_sem=d_send.at[way, owner, c],
            recv_sem=d_recv.at[owner, c],
            device_id={"grp": g + 1 if way == 0 else g - 1},
            device_id_type=MESH,
        )

    def d_arrived(owner, c):
        piece = pl.ds(c * part, part)
        pltpu.make_async_remote_copy(
            src_ref=d_all.at[owner, piece],
            dst_ref=d_all.at[owner, piece],
            send_sem=d_send.at[0, owner, c],
            recv_sem=d_recv.at[owner, c],
            device_id={"leaf": twin},
            device_id_type=MESH,
        ).wait_recv()

    up, down = g < groups - 1, g > 0

    for step in range(1, groups):
        root_z(step).start()
    for step in list(range(1, chips)) + [0]:
        root_plane(step, g, True).start()
    for c in range(CHUNKS):
        @pl.when(up)
        def _():
            d_copy(0, g, c, True).start()

        @pl.when(down)
        def _():
            d_copy(1, g, c, True).start()

    def forward_root(step):
        for owner, there in ((g - step, g - step >= 0), (g + step, g + step < groups)):
            @pl.when(there)
            def _():
                root_arrived(leaf * groups + owner)
                for hop in list(range(1, chips)) + [0]:
                    root_plane(hop, owner, False).start()

    def forward_d(step):
        for c in range(CHUNKS):
            for way, owner, there, onward in (
                (0, g - step, g - step >= 0, up),
                (1, g + step, g + step < groups, down),
            ):
                @pl.when(there)
                def _():
                    d_arrived(owner, c)

                    @pl.when(onward)
                    def _():
                        d_copy(way, owner, c, False).start()

    row_at = lax.broadcasted_iota(jnp.int32, (listed * B, 1), 0)
    col_at = lax.broadcasted_iota(jnp.int32, (1, listed * B), 1)
    start = jnp.zeros((listed * B, 1), jnp.int32)
    keep = jnp.zeros((1, listed * B), jnp.int32)
    for k in range(listed):
        met = valid[0, k]
        column = jnp.where(met > 0, tiles[0, k] * B - k * B, -(2 * total) - listed * B)
        start = jnp.where(row_at // B == k, column, start)
        keep = jnp.where(col_at // B == k, met, keep)
    spot = lax.broadcasted_iota(jnp.int32, (listed * B, total), 1)
    pick = (start + row_at == spot).astype(F32)
    chosen = jnp.max(pick, axis=0, keepdims=True) > 0
    pick = pick.astype(BF16)

    copy_d.wait()
    d_own = d_all[g]
    d_half = halves(d_own)
    copy_f.wait()
    f_half = halves(f_all[...])
    product = dot3(d_half, f_half, True)
    product = jnp.where(keep > 0, product, 0.0)
    spread = tuple(dot(x, pick).astype(BF16) for x in halves(product))

    copy_r.wait()
    for step in range(1, groups):
        forward_root(step)
    for step in range(1, groups - 1):
        forward_d(step)
    order = [0]
    for away in range(1, groups):
        order += [away, -away]
    for away in order:
        owner = g + away
        @pl.when(jnp.logical_and(owner >= 0, owner < groups))
        def _():
            for step in range(1, chips):
                root_arrived(leaf_of(step) * groups + owner)
                root_twin(step, owner).start()
    for away in order:
        owner = g + away
        @pl.when(jnp.logical_and(owner >= 0, owner < groups))
        def _():
            for step in range(chips):
                other = lax.rem(chip + step, chips) * 2 + (1 - core)
                root_arrived(other * groups + owner)

    cross = jnp.zeros((rows, listed * B), F32)
    block = min(total, 512)
    for n in range(total // block):
        cols = slice(n * block, (n + 1) * block)
        source = root_all[:, :, cols].reshape(total, block)
        y = dot3(spread, halves(source))
        yh, yl = halves(jnp.where(chosen[:, cols], y, 0.0))
        cross = cross - (dot(yh, pick[:, cols], True) + dot(yl, pick[:, cols], True))
    cross_out[...] = cross
    q = halves(d_own - dot3(halves(cross), f_half))

    def close(owner):
        closing[owner] = dot3(q, halves(d_all[owner]), True)

    close(g)
    for step in range(1, groups):
        if step == groups - 1:
            forward_d(step)
        for owner, there in ((g - step, g - step >= 0), (g + step, g + step < groups)):
            @pl.when(there)
            def _():
                close(owner)
    for h in range(groups):
        closing_out[:, h * rows:(h + 1) * rows] = closing[h]

    for step in range(1, groups):
        root_z(step).wait_send()
    for h in range(groups):
        for way, goes in (
            (0, jnp.logical_and(h <= g, up)),
            (1, jnp.logical_and(h >= g, down)),
        ):
            @pl.when(goes)
            def _():
                for c in range(CHUNKS):
                    d_copy(way, h, c, False).wait_send()
        for step in range(chips):
            root_plane(step, h, False).wait_send()
        for step in range(1, chips):
            root_twin(step, h).wait_send()


def on_device(root, tiles, valid, factor, diag_t):
    leaves, groups = lax.axis_size("leaf"), lax.axis_size("grp")
    rows, width = diag_t.shape[1:]
    part, total = root.shape
    deep = factor.shape[1]
    smem = pl.BlockSpec(memory_space=pltpu.SMEM)
    anywhere = pl.BlockSpec(memory_space=pl.ANY)
    vmem = pl.BlockSpec(memory_space=pltpu.VMEM)
    dma = pltpu.SemaphoreType.DMA
    cross, closing = pl.pallas_call(
        functools.partial(kernel, leaves, groups),
        out_shape=(
            pltpu.VMEM((rows, deep), F32),
            pltpu.VMEM((rows, groups * rows), F32),
        ),
        in_specs=[smem, smem, anywhere, anywhere, anywhere],
        out_specs=(vmem, vmem),
        scratch_shapes=[
            pltpu.VMEM((groups, rows, width), F32),
            pltpu.VMEM((leaves * groups, part, total), F32),
            pltpu.VMEM((deep, width), F32),
            pltpu.VMEM((groups, rows, rows), F32),
            dma((3,)),
            dma((leaves * groups,)),
            dma((groups,)),
            dma((leaves // 2, groups)),
            dma((leaves // 2, groups)),
            dma((groups, CHUNKS)),
            dma((2, groups, CHUNKS)),
        ],
        compiler_params=pltpu.CompilerParams(
            collective_id=0, has_side_effects=True, vmem_limit_bytes=56 * 1024 * 1024
        ),
        name="selected_inverse",
    )(tiles, valid, root, factor[0], diag_t[0])
    return cross[None], closing[None]


def solution(mesh):
    in_specs = (
        P(("leaf", "grp"), None),
        P("leaf", None),
        P("leaf", None),
        P("leaf", None, None),
        P("leaf", "grp", None),
    )
    out_specs = (P("leaf", "grp", None), P("leaf", "grp", None))
    return jax.shard_map(
        on_device, mesh=mesh, in_specs=in_specs, out_specs=out_specs, check_vma=False
    )
```

```python
import functools

import jax
import jax.numpy as jnp
from jax import lax
from jax.experimental import pallas as pl
from jax.experimental.pallas import tpu as pltpu
from jax.sharding import PartitionSpec as P

B = 64
CHUNKS = 4
FIRST = 2
MESH = pl.DeviceIdType.MESH
BF16 = jnp.bfloat16
F32 = jnp.float32


def halves(x):
    high = x.astype(BF16)
    return high, (x - high.astype(F32)).astype(BF16)


def dot(a, b, transpose_b=False):
    dims = (((1,), (1 if transpose_b else 0,)), ((), ()))
    return lax.dot_general(a, b, dims, preferred_element_type=F32)


def dot3(a, b, transpose_b=False):
    (ah, al), (bh, bl) = a, b
    return dot(ah, bh, transpose_b) + (dot(al, bh, transpose_b) + dot(ah, bl, transpose_b))


def kernel(
    leaves, groups,
    tiles, valid, root, factor, diag_t, cross_out, closing_out,
    d_all, root_all, f_all, closing,
    local_sem, root_recv, root_zsend, root_psend, root_tsend, d_recv, d_send,
):
    leaf = lax.axis_index("leaf")
    g = lax.axis_index("grp")
    chips = leaves // 2
    chip, core = leaf // 2, lax.rem(leaf, 2)
    twin = chip * 2 + (1 - core)
    listed = tiles.shape[1]
    rows, width = diag_t.shape
    total = root.shape[1]
    part = rows // CHUNKS

    def leaf_of(step):
        return lax.rem(chip + step, chips) * 2 + core

    barrier = pltpu.get_barrier_semaphore()

    for step in range(1, groups):
        pl.semaphore_signal(
            barrier, inc=1, device_id={"grp": lax.rem(g + step, groups)}, device_id_type=MESH
        )
    pl.semaphore_signal(barrier, inc=1, device_id={"leaf": twin}, device_id_type=MESH)
    for step in range(1, chips):
        pl.semaphore_signal(barrier, inc=1, device_id={"leaf": leaf_of(step)}, device_id_type=MESH)

    mine = leaf * groups + g
    copy_d = pltpu.make_async_copy(diag_t, d_all.at[g], local_sem.at[0])
    copy_f = pltpu.make_async_copy(factor, f_all, local_sem.at[1])
    copy_r = pltpu.make_async_copy(root, root_all.at[mine], local_sem.at[2])
    copy_d.start()
    copy_f.start()
    copy_r.start()
    pl.semaphore_wait(barrier, groups - 1 + chips)

    def root_z(step):
        return pltpu.make_async_remote_copy(
            src_ref=root,
            dst_ref=root_all.at[mine],
            send_sem=root_zsend.at[step],
            recv_sem=root_recv.at[mine],
            device_id={"grp": lax.rem(g + step, groups)},
            device_id_type=MESH,
        )

    def root_plane(step, owner, own):
        slot = leaf * groups + owner
        return pltpu.make_async_remote_copy(
            src_ref=root if own else root_all.at[slot],
            dst_ref=root_all.at[slot],
            send_sem=root_psend.at[step, owner],
            recv_sem=root_recv.at[slot],
            device_id={"leaf": twin if step == 0 else leaf_of(step)},
            device_id_type=MESH,
        )

    def root_twin(step, owner):
        slot = leaf_of(step) * groups + owner
        return pltpu.make_async_remote_copy(
            src_ref=root_all.at[slot],
            dst_ref=root_all.at[slot],
            send_sem=root_tsend.at[step, owner],
            recv_sem=root_recv.at[slot],
            device_id={"leaf": twin},
            device_id_type=MESH,
        )

    def root_arrived(slot):
        pltpu.make_async_remote_copy(
            src_ref=root_all.at[slot],
            dst_ref=root_all.at[slot],
            send_sem=root_tsend.at[0, 0],
            recv_sem=root_recv.at[slot],
            device_id={"leaf": twin},
            device_id_type=MESH,
        ).wait_recv()

    def d_copy(way, owner, c, own):
        piece = pl.ds(c * part, part)
        return pltpu.make_async_remote_copy(
            src_ref=diag_t.at[piece] if own else d_all.at[owner, piece],
            dst_ref=d_all.at[owner, piece],
            send_sem=d_send.at[way, owner, c],
            recv_sem=d_recv.at[owner, c],
            device_id={"grp": g + 1 if way == 0 else g - 1},
            device_id_type=MESH,
        )

    def d_arrived(owner, c):
        piece = pl.ds(c * part, part)
        pltpu.make_async_remote_copy(
            src_ref=d_all.at[owner, piece],
            dst_ref=d_all.at[owner, piece],
            send_sem=d_send.at[0, owner, c],
            recv_sem=d_recv.at[owner, c],
            device_id={"leaf": twin},
            device_id_type=MESH,
        ).wait_recv()

    up, down = g < groups - 1, g > 0

    for step in range(1, groups):
        root_z(step).start()
    for step in list(range(1, chips)) + [0]:
        root_plane(step, g, True).start()
    def first_d(some):
        for c in some:
            @pl.when(up)
            def _():
                d_copy(0, g, c, True).start()

            @pl.when(down)
            def _():
                d_copy(1, g, c, True).start()

    first_d(range(FIRST))

    def forward_root(step):
        for owner, there in ((g - step, g - step >= 0), (g + step, g + step < groups)):
            @pl.when(there)
            def _():
                root_arrived(leaf * groups + owner)
                for hop in list(range(1, chips)) + [0]:
                    root_plane(hop, owner, False).start()

    def forward_d(step):
        for c in range(CHUNKS):
            for way, owner, there, onward in (
                (0, g - step, g - step >= 0, up),
                (1, g + step, g + step < groups, down),
            ):
                @pl.when(there)
                def _():
                    d_arrived(owner, c)

                    @pl.when(onward)
                    def _():
                        d_copy(way, owner, c, False).start()

    copy_r.wait()
    for step in range(1, groups):
        forward_root(step)
    first_d(range(FIRST, CHUNKS))

    row_at = lax.broadcasted_iota(jnp.int32, (listed * B, 1), 0)
    col_at = lax.broadcasted_iota(jnp.int32, (1, listed * B), 1)
    start = jnp.zeros((listed * B, 1), jnp.int32)
    keep = jnp.zeros((1, listed * B), jnp.int32)
    for k in range(listed):
        met = valid[0, k]
        column = jnp.where(met > 0, tiles[0, k] * B - k * B, -(2 * total) - listed * B)
        start = jnp.where(row_at // B == k, column, start)
        keep = jnp.where(col_at // B == k, met, keep)
    spot = lax.broadcasted_iota(jnp.int32, (listed * B, total), 1)
    pick = (start + row_at == spot).astype(F32)
    chosen = jnp.max(pick, axis=0, keepdims=True) > 0
    pick = pick.astype(BF16)

    copy_d.wait()
    d_own = d_all[g]
    d_half = halves(d_own)
    copy_f.wait()
    f_half = halves(f_all[...])
    product = dot3(d_half, f_half, True)
    product = jnp.where(keep > 0, product, 0.0)
    spread = tuple(dot(x, pick).astype(BF16) for x in halves(product))

    forward_d(1)
    order = [0]
    for away in range(1, groups):
        order += [away, -away]
    for away in order:
        owner = g + away
        @pl.when(jnp.logical_and(owner >= 0, owner < groups))
        def _():
            for step in range(1, chips):
                root_arrived(leaf_of(step) * groups + owner)
                root_twin(step, owner).start()
    for step in range(2, groups - 1):
        forward_d(step)
    for away in order:
        owner = g + away
        @pl.when(jnp.logical_and(owner >= 0, owner < groups))
        def _():
            for step in range(chips):
                other = lax.rem(chip + step, chips) * 2 + (1 - core)
                root_arrived(other * groups + owner)

    cross = jnp.zeros((rows, listed * B), F32)
    block = min(total, 512)
    for n in range(total // block):
        cols = slice(n * block, (n + 1) * block)
        source = root_all[:, :, cols].reshape(total, block)
        y = dot3(spread, halves(source))
        yh, yl = halves(jnp.where(chosen[:, cols], y, 0.0))
        cross = cross - (dot(yh, pick[:, cols], True) + dot(yl, pick[:, cols], True))
    cross_out[...] = cross
    q = halves(d_own - dot3(halves(cross), f_half))

    def close(owner):
        closing[owner] = dot3(q, halves(d_all[owner]), True)

    close(g)
    for step in range(1, groups):
        if step == groups - 1:
            forward_d(step)
        for owner, there in ((g - step, g - step >= 0), (g + step, g + step < groups)):
            @pl.when(there)
            def _():
                close(owner)
    for h in range(groups):
        closing_out[:, h * rows:(h + 1) * rows] = closing[h]

    for step in range(1, groups):
        root_z(step).wait_send()
    for h in range(groups):
        for way, goes in (
            (0, jnp.logical_and(h <= g, up)),
            (1, jnp.logical_and(h >= g, down)),
        ):
            @pl.when(goes)
            def _():
                for c in range(CHUNKS):
                    d_copy(way, h, c, False).wait_send()
        for step in range(chips):
            root_plane(step, h, False).wait_send()
        for step in range(1, chips):
            root_twin(step, h).wait_send()


def on_device(root, tiles, valid, factor, diag_t):
    leaves, groups = lax.axis_size("leaf"), lax.axis_size("grp")
    rows, width = diag_t.shape[1:]
    part, total = root.shape
    deep = factor.shape[1]
    smem = pl.BlockSpec(memory_space=pltpu.SMEM)
    anywhere = pl.BlockSpec(memory_space=pl.ANY)
    vmem = pl.BlockSpec(memory_space=pltpu.VMEM)
    dma = pltpu.SemaphoreType.DMA
    cross, closing = pl.pallas_call(
        functools.partial(kernel, leaves, groups),
        out_shape=(
            pltpu.VMEM((rows, deep), F32),
            pltpu.VMEM((rows, groups * rows), F32),
        ),
        in_specs=[smem, smem, anywhere, anywhere, anywhere],
        out_specs=(vmem, vmem),
        scratch_shapes=[
            pltpu.VMEM((groups, rows, width), F32),
            pltpu.VMEM((leaves * groups, part, total), F32),
            pltpu.VMEM((deep, width), F32),
            pltpu.VMEM((groups, rows, rows), F32),
            dma((3,)),
            dma((leaves * groups,)),
            dma((groups,)),
            dma((leaves // 2, groups)),
            dma((leaves // 2, groups)),
            dma((groups, CHUNKS)),
            dma((2, groups, CHUNKS)),
        ],
        compiler_params=pltpu.CompilerParams(
            collective_id=0, has_side_effects=True, vmem_limit_bytes=56 * 1024 * 1024
        ),
        name="selected_inverse",
    )(tiles, valid, root, factor[0], diag_t[0])
    return cross[None], closing[None]


def solution(mesh):
    in_specs = (
        P(("leaf", "grp"), None),
        P("leaf", None),
        P("leaf", None),
        P("leaf", None, None),
        P("leaf", "grp", None),
    )
    out_specs = (P("leaf", "grp", None), P("leaf", "grp", None))
    return jax.shard_map(
        on_device, mesh=mesh, in_specs=in_specs, out_specs=out_specs, check_vma=False
    )
```
